32 devices in a mesh: ep: 4 (over z), tp: 4 (over y, x), dp: 2 (over core).
Axes of the slice: x: 2, y: 2, z: 4, core: 2. Of those that a mesh axis runs over, the one named last changes fastest.
Arguments:
- x_in: float32 [16384, 768], P(('ep', 'tp', 'dp')), may hold values from -6 to 6
- grad_out: float32 [16384, 768], P(('ep', 'tp', 'dp')), may hold values from -6 to 6
- norm1_gain: float32 [768], replicated, may hold values from 0.5 to 1.5
- qkv_weight: bfloat16 [768, 2304], P('dp', 'tp'), may hold values from -0.21875 to 0.21875
- out_weight: bfloat16 [768, 768], P('tp', 'dp'), may hold values from -2.5 to 2.5
- bias_table: float32 [32, 12], replicated, may hold values from -4 to 4
- norm2_gain: float32 [768], replicated, may hold values from 0.5 to 1.5
- router_weight: bfloat16 [768, 4], replicated, may hold values from -0.15625 to 0.15625
- expert_in: bfloat16 [4, 768, 3072], P('ep', None, ('tp', 'dp')), may hold values from -0.21875 to 0.21875
- expert_out: bfloat16 [4, 3072, 768], P('ep', ('tp', 'dp')), may hold values from -0.4375 to 0.4375
- lengths: int32 [8, 4], P(('ep', 'dp')), may hold values from 1 to 1024, 2048 in all within a row
- routes: int32 [16384, 1], P(('ep', 'tp', 'dp')), may hold values from 0 to 3; in each aligned block of 512 rows (0 to 511, 512 to 1023, ...) at most 256 rows name the same one
Outputs:
- out: float32 [16384, 768], P(('ep', 'tp', 'dp'))
- grad_in: float32 [16384, 768], P(('ep', 'tp', 'dp'))
- grad_norm1: float32 [768], replicated
- grad_qkv_weight: float32 [768, 2304], P('dp', 'tp')
- grad_out_weight: float32 [768, 768], P('tp', 'dp')
- grad_bias_table: float32 [32, 12], replicated
- grad_norm2: float32 [768], replicated
- grad_router: float32 [768, 4], replicated
- grad_expert_in: float32 [4, 768, 3072], P('ep', None, ('tp', 'dp'))
- grad_expert_out: float32 [4, 3072, 768], P('ep', ('tp', 'dp'))
The draws below stay inside these ranges and needn't reach their ends.
Inputs may be any that keep to these rules, and one draw needn't show every extreme that they name: `lengths`: each row sums to 2048 and its largest length is exactly 1024. `routes`: within each aligned block of 512 rows (the tokens of one device) no expert is named by more than 256 rows, a bound that some block reaches.
All inputs are finite; a program needn't handle non-finite values.
Results may differ from the reference program's by a relative error of at most 0.023.
Values may be sent and summed in bfloat16 or wider, within the bound.
A program may use at most 192 MiB of HBM per device.

```python
import math
from functools import partial
import jax
import jax.numpy as jnp
import numpy as np
from jax import lax

D = 768
HEADS = 12
HEAD = 64
FF = 3072
BUCKETS = 32
TOK_DEV = 512
NSEQ = 4
EXPERTS = 4
CAP = 256
SPAN = 2048
GROUPS = 8
TOKENS = 16384
MAXLEN = 1024


def steps_of(own_key, shape, pieces, low, top_value):
    loudness, own = 1.0, jax.random.fold_in(own_key, 6)
    for dim, parts in pieces:
        heights = jnp.exp(jax.random.uniform(jax.random.fold_in(own, dim), (parts,), jnp.float32, low / len(pieces), top_value / len(pieces)))
        loudness = loudness * jnp.repeat(heights, shape[dim] // parts).reshape([-1 if axis == dim else 1 for axis in range(len(shape))])
    return loudness


def split_up(count, total, limit, skew):
    loads = [(1 << 20) // math.isqrt(rank ** skew) + 1 for rank in range(2, count + 1)]
    surplus, holding = total - limit - (count - 1), [1] * (count - 1)
    while surplus > 0:
        free = [i for i in range(count - 1) if holding[i] < limit]
        whole, budget = sum([loads[i] for i in free]), surplus
        for i in free:
            more = min(limit - holding[i], max(1, budget * loads[i] // whole), surplus)
            holding[i] = holding[i] + more
            surplus = surplus - more
    return np.array([limit] + holding)


def uneven_parts(own_key, count, total, reach, lean):
    if count == 2:
        one = jax.random.randint(own_key, (), max(1, total - reach), min(reach, total - 1) + 1)
        return jnp.stack([one, total - one])
    sizes = jnp.asarray(split_up(count, total, reach, lean), jnp.int32)
    pairs = (count - 1) // 2
    donor, receiver = sizes[1:1 + 2 * pairs:2], sizes[2:2 + 2 * pairs:2]
    margin = jnp.minimum(donor - 1, reach - receiver)
    moved = jax.random.randint(jax.random.fold_in(own_key, 1), (pairs,), 0, 1 << 20) % (margin + 1)
    sizes = sizes.at[1:1 + 2 * pairs:2].set(donor - moved).at[2:2 + 2 * pairs:2].set(receiver + moved)
    return sizes[jax.random.permutation(jax.random.fold_in(own_key, 2), count)]


def shared_out(key, own, number, rows, amount, top, reach, slope):
    order = jax.random.permutation(key, amount)
    packed, usual = load_shares(amount, rows * top, reach, slope, True), load_shares(amount, rows * top, reach, slope, False)
    places = jnp.arange(amount)

    def named(sizes, offset_by):
        used = int((sizes > 0).sum())
        fixed = max(1, used // 4)
        moved = fixed + (places - fixed + offset_by * (used - fixed)) % max(1, amount - fixed)
        return jnp.zeros((amount,), jnp.int32).at[order[jnp.where(places < fixed, places, moved)]].set(jnp.asarray(sizes, jnp.int32))

    sizes = jnp.where(number % 4 == 0, named(packed, number // 4), named(usual, number - number // 4 - 1))
    mixed = jax.random.permutation(jax.random.fold_in(own, 3), amount)
    source_of, sink = mixed[0:amount // 2 * 2:2], mixed[1:amount // 2 * 2:2]
    room = jnp.minimum(sizes[source_of] - 1, reach - sizes[sink]) // 2
    room = jnp.where((source_of == order[0]) | (sink == order[0]) | (sizes[sink] == 0), 0, jnp.maximum(room, 0))
    moved = jax.random.randint(jax.random.fold_in(own, 4), (amount // 2,), 0, 1 << 20) % (room + 1)
    sizes = sizes.at[source_of].add(-moved).at[sink].add(moved)
    members = jnp.searchsorted(jnp.cumsum(sizes), jnp.arange(rows * top), side="right").astype(jnp.int32)
    listing = members.reshape(top, rows).T
    listing = listing[jax.random.permutation(jax.random.fold_in(own, 1), rows)]
    offset_by = jax.random.randint(jax.random.fold_in(own, 2), (rows, 1), 0, top)
    return jnp.take_along_axis(listing, (jnp.arange(top)[None, :] + offset_by) % top, axis=1)


def load_shares(count, total, reach, slope, full):
    portions = [(1 << 20) // math.isqrt(rank ** slope) + 1 for rank in range(1, count + 1)]
    largest = reach if full else min(reach, max(-(-total // count), total * portions[0] // sum(portions)))
    least = 1 if total - largest >= count - 1 else 0
    given, spare = [largest] + [least] * (count - 1), total - largest - least * (count - 1)
    while spare > 0:
        candidates = [i for i in range(1, count) if given[i] < largest] or [i for i in range(1, count) if given[i] < reach]
        whole, budget = sum([portions[i] for i in candidates]), spare
        for i in candidates:
            more = min(reach - given[i], max(1, budget * portions[i] // whole), spare)
            given[i] = given[i] + more
            spare = spare - more
    return np.array(given)


def normal_values(rng, dims, scale, reach, shards=(), held_as=jnp.bfloat16):
    drawn = jax.random.normal(rng, dims, jnp.float32) * scale
    if len(shards) > 0:
        drawn = steps_of(rng, dims, shards, -0.22, 0.18) * drawn
    return jnp.clip(drawn, min=-reach, max=reach).astype(held_as)


def setup_inputs(seed: int = 0) -> dict:
    key_list = jax.random.split(jax.random.key(seed), 13)
    x_in = normal_values(key_list[0], (TOKENS, D), 1.0, 6.0, ((0, 32),), jnp.float32)
    grad_out = normal_values(key_list[1], (TOKENS, D), 1.0, 6.0, ((0, 32),), jnp.float32)
    norm1_gain = jnp.clip(1.0 + 0.1 * jax.random.normal(key_list[2], (D,), jnp.float32), 0.5, 1.5)
    qkv_weight = normal_values(key_list[3], (D, 3 * HEADS * HEAD), D ** -0.5, 0.21875, ((0, 2), (1, 4)))
    out_weight = normal_values(key_list[4], (HEADS * HEAD, D), (HEADS * HEAD * 8 // MAXLEN) ** -0.5, 2.5, ((0, 4), (1, 2)))
    bias_table = normal_values(key_list[5], (BUCKETS, HEADS), 1.0, 4.0, (), jnp.float32)
    norm2_gain = jnp.clip(1.0 + 0.1 * jax.random.normal(key_list[6], (D,), jnp.float32), 0.5, 1.5)
    router_weight = normal_values(key_list[7], (D, EXPERTS), (2 * D) ** -0.5, 0.15625)
    expert_in = normal_values(key_list[8], (EXPERTS, D, FF), D ** -0.5, 0.21875, ((0, 4), (2, 8)))
    expert_out = normal_values(key_list[9], (EXPERTS, FF, D), (max(1, FF // (EXPERTS * EXPERTS))) ** -0.5, 0.4375, ((0, 4), (1, 8)))
    lengths = jax.vmap(lambda own: uneven_parts(own, NSEQ, SPAN, MAXLEN, 2))(jax.random.split(key_list[10], GROUPS)).reshape((GROUPS, NSEQ)).astype(jnp.int32)
    routes_keys = jax.random.split(jax.random.fold_in(key_list[11], 1), TOKENS // TOK_DEV)
    routes_turns = jax.random.permutation(jax.random.fold_in(key_list[11], 3), TOKENS // TOK_DEV)
    routes = jax.vmap(lambda own, number: shared_out(jax.random.fold_in(key_list[11], 2), own, number, TOK_DEV, EXPERTS, 1, CAP, 2))(routes_keys, routes_turns).reshape((TOKENS, 1))
    return {"x_in": x_in, "grad_out": grad_out, "norm1_gain": norm1_gain, "qkv_weight": qkv_weight, "out_weight": out_weight, "bias_table": bias_table, "norm2_gain": norm2_gain, "router_weight": router_weight, "expert_in": expert_in, "expert_out": expert_out, "lengths": lengths, "routes": routes}


@jax.custom_vjp
def low(v):
    return lax.optimization_barrier(v.astype(jnp.bfloat16)).astype(jnp.float32)

@jax.custom_vjp
def low_back(v):
    return v

def low_keep(v):
    return (low(v), None)

def low_pass(kept, grad):
    return (grad,)

def back_keep(v):
    return (v, None)

def back_low(kept, grad):
    return (low(grad),)
low.defvjp(low_keep, low_pass)
low_back.defvjp(back_keep, back_low)
EPS = 1e-06
NEG = -1e+30
THRESHOLDS = (12, 16, 23, 32, 46, 64, 91)
GELU_C = 0.7978845608028654
HIGH = lax.Precision.HIGHEST

def rel_bucket(offsets):
    distance = jnp.abs(offsets)
    bucket = jnp.minimum(distance, 8) + 16 * (offsets > 0).astype(jnp.int32)
    for threshold in THRESHOLDS:
        bucket = bucket + (distance >= threshold).astype(jnp.int32)
    return bucket

def segment_ids(lengths_row, row_count):
    seq_ends = jnp.cumsum(lengths_row, dtype=jnp.int32)
    positions = jnp.arange(row_count, dtype=jnp.int32)
    return lax.optimization_barrier(jnp.sum((positions[:, None] >= seq_ends[None, :-1]).astype(jnp.int32), axis=1, dtype=jnp.int32))

def gelu_tanh(inputs):
    return 0.5 * inputs * (1.0 + jnp.tanh(GELU_C * (inputs + 0.044715 * inputs * inputs * inputs)))

def rms_scale(values, gain_vector):
    return values * lax.rsqrt(lax.optimization_barrier(jnp.mean(values * values, axis=-1, keepdims=True)) + EPS) * gain_vector

def softmax_rows(scores):
    shifted = scores - lax.optimization_barrier(jnp.max(scores, axis=-1, keepdims=True))
    weights = jnp.exp(shifted)
    return weights / lax.optimization_barrier(jnp.sum(weights, axis=-1, keepdims=True))

def group_forward(weights_all, x_rows, lengths_row, routes_rows):
    gain_one, qkv_w, out_w, table, gain_two, router_w, weight_in_all, weight_out_all = weights_all
    group_span = x_rows.shape[0]
    normed = low(rms_scale(x_rows, gain_one))
    projected = jnp.dot(normed, qkv_w, precision=HIGH)
    qkv = low_back(low(projected)).reshape(group_span, HEADS, 3, HEAD)
    query_rows, key_rows, value_rows = (qkv[:, :, 0], qkv[:, :, 1], qkv[:, :, 2])
    sequence = segment_ids(lengths_row, group_span)
    block_rows = min(512, group_span)
    positions = jnp.arange(group_span, dtype=jnp.int32)

    def attend(row_start):
        rows_here = lax.dynamic_slice_in_dim(query_rows, row_start, block_rows, 0)
        row_pos = row_start + jnp.arange(block_rows, dtype=jnp.int32)
        row_seq = lax.dynamic_slice_in_dim(sequence, row_start, block_rows, 0)
        scores = jnp.einsum('qhe,khe->hqk', rows_here, key_rows, precision=HIGH) * HEAD ** (-0.5)
        buckets = rel_bucket(positions[None, :] - row_pos[:, None])
        bias = jnp.take(table, buckets, axis=0)
        scores = scores + jnp.transpose(bias, (2, 0, 1))
        same_seq = (row_seq[:, None] == sequence[None, :])[None]
        scores = low_back(jnp.where(same_seq, scores, NEG))
        probs = softmax_rows(scores)
        return jnp.einsum('hqk,khe->qhe', low(probs), value_rows, precision=HIGH)
    starts = jnp.arange(group_span // block_rows, dtype=jnp.int32) * block_rows
    attended = lax.map(jax.checkpoint(attend), starts).reshape(group_span, HEADS * HEAD)
    attended = low_back(low(attended))
    attn = low_back(jnp.dot(attended, out_w, precision=HIGH))
    hidden = x_rows + attn
    normed2 = low(rms_scale(hidden, gain_two))
    logits = low_back(jnp.dot(normed2, router_w, precision=HIGH))
    router = softmax_rows(logits)
    route_hot = (routes_rows[:, 0][:, None] == jnp.arange(EXPERTS, dtype=jnp.int32)[None, :]).astype(jnp.float32)
    gate = lax.optimization_barrier(jnp.sum(router * route_hot, axis=1, keepdims=True))
    sent = low_back(normed2)

    def expert_apply(mixed, expert_index):
        pre_act = low_back(jnp.dot(sent, weight_in_all[expert_index], precision=HIGH))
        active = low(gelu_tanh(pre_act))
        result = low_back(low(jnp.dot(active, weight_out_all[expert_index], precision=HIGH)))
        chosen = lax.dynamic_slice_in_dim(route_hot, expert_index, 1, 1)
        return (mixed + result * chosen, None)
    mixed, unused = lax.scan(jax.checkpoint(expert_apply), jnp.zeros(x_rows.shape, jnp.float32), jnp.arange(EXPERTS, dtype=jnp.int32))
    return hidden + gate * mixed

def reference(x_in, grad_out, norm1_gain, qkv_weight, out_weight, bias_table, norm2_gain, router_weight, expert_in, expert_out, lengths, routes):
    weights_all = (norm1_gain, qkv_weight.astype(jnp.float32), out_weight.astype(jnp.float32), bias_table, norm2_gain, router_weight.astype(jnp.float32), expert_in.astype(jnp.float32), expert_out.astype(jnp.float32))

    def whole(weights_now, x_all):
        group_step = jax.checkpoint(partial(group_forward, weights_now))
        rows_all = x_all.reshape(GROUPS, SPAN, D)
        routes_all = routes.reshape(GROUPS, SPAN, 1)
        result = lax.map(lambda items: group_step(items[0], items[1], items[2]), (rows_all, lengths, routes_all))
        return result.reshape(TOKENS, D)
    out, pull = jax.vjp(whole, weights_all, x_in)
    grads, grad_in = pull(grad_out)
    return (out, grad_in, grads[0], grads[1], grads[2], grads[3], grads[4], grads[5], grads[6], grads[7])
```

```python
import functools

import jax
import jax.numpy as jnp
from jax import lax
from jax.experimental import pallas as pl
from jax.experimental.pallas import tpu as pltpu
from jax.sharding import PartitionSpec as P

HEAD = 64


EPS = 1e-06
NEG = -1e30
STEP_EDGES = (1, 2, 3, 4, 5, 6, 7, 8, 12, 16, 23, 32, 46, 64, 91)
GELU_C = 0.7978845608028654


def segment_ids(lengths_row, row_count):
    seq_ends = jnp.cumsum(lengths_row, dtype=jnp.int32)
    positions = jnp.arange(row_count, dtype=jnp.int32)
    return jnp.sum(
        (positions[:, None] >= seq_ends[None, :-1]).astype(jnp.int32), axis=1, dtype=jnp.int32
    )


def gelu_tanh(inputs):
    return 0.5 * inputs * (1.0 + jnp.tanh(GELU_C * (inputs + 0.044715 * inputs * inputs * inputs)))


def norm_apply(values, gain_vector):
    return values * lax.rsqrt(jnp.mean(values * values, axis=-1, keepdims=True) + EPS) * gain_vector


def contract_rows(left, right):
    return lax.dot_general(
        left, right, (((0,), (0,)), ((), ())), preferred_element_type=jnp.float32
    )


def contract_cols(left, right):
    return lax.dot_general(
        left, right, (((1,), (1,)), ((), ())), preferred_element_type=jnp.float32
    )


def row_product(left, right, transposed):

    def product(row_start, row_count):
        if transposed:
            return contract_cols(left, right)
        return jnp.dot(left, right, preferred_element_type=jnp.float32)

    return product


def split_columns(values):
    return lax.all_to_all(values, "dp", split_axis=1, concat_axis=0, tiled=True)


def gather_group(values):
    return lax.all_gather(values, "tp", axis=0, tiled=True)


def sum_halves(product, row_count):
    return lax.psum_scatter(
        product(jnp.int32(0), row_count * lax.axis_size("dp")),
        "dp",
        scatter_dimension=0,
        tiled=True,
    )


def gather_halves(values):
    return lax.all_gather(values, "dp", axis=0, tiled=True)


def sum_blocks(product, row_count):
    return lax.psum_scatter(
        product(jnp.int32(0), lax.axis_size("tp") * row_count).astype(jnp.bfloat16),
        "tp",
        scatter_dimension=0,
        tiled=True,
    ).astype(jnp.float32)


def join_rows(values):
    return lax.all_to_all(
        values.astype(jnp.bfloat16), "dp", split_axis=0, concat_axis=1, tiled=True
    ).astype(values.dtype)


def send_experts(values):
    return lax.all_to_all(values, "ep", split_axis=0, concat_axis=0, tiled=True)


def return_tokens(values):
    return lax.all_to_all(values, "ep", split_axis=0, concat_axis=0, tiled=True)


def rel_bucket(offsets):
    distance = jnp.abs(offsets)
    bucket = jnp.where(offsets > 0, 16, 0)
    for edge in STEP_EDGES:
        bucket = bucket + (distance >= edge).astype(jnp.int32)
    return bucket


def tile_offsets(block_rows):
    keys = jnp.arange(3 * block_rows, dtype=jnp.int32)[:, None] - block_rows
    return keys - jnp.arange(block_rows, dtype=jnp.int32)[None, :]


def bias_tiles(table_heads, block_rows):
    offsets = tile_offsets(block_rows)[None]
    distance = jnp.abs(offsets)
    ahead = offsets > 0
    near = jnp.zeros((1, 1, 1), jnp.float32) + table_heads[:, 0][:, None, None]
    for index, edge in enumerate(STEP_EDGES):
        step = jnp.where(
            ahead,
            table_heads[:, 17 + index][:, None, None],
            table_heads[:, 1 + index][:, None, None],
        )
        near = jnp.where(distance >= edge, step, near)
    heads = table_heads.shape[0]
    flat = jnp.ones((1, block_rows, block_rows), jnp.float32)
    return jnp.concatenate(
        [
            table_heads[:, 15][:, None, None] * flat,
            near,
            table_heads[:, 31][:, None, None] * flat,
        ],
        axis=1,
    ).reshape(heads, 5, block_rows, block_rows)


def table_gradient(tile_sums, block_rows):
    heads = tile_sums.shape[0]
    near = tile_sums[:, 1:4].reshape(heads, 3 * block_rows, block_rows)
    buckets = rel_bucket(tile_offsets(block_rows))
    sums = [
        jnp.sum(jnp.where(buckets[None] == index, near, 0.0), axis=(1, 2))
        for index in range(32)
    ]
    sums[15] = sums[15] + jnp.sum(tile_sums[:, 0], axis=(1, 2))
    sums[31] = sums[31] + jnp.sum(tile_sums[:, 4], axis=(1, 2))
    return jnp.stack(sums, axis=1)


def tile_ranges(lengths_row, sequence, block_rows):
    ends = jnp.cumsum(lengths_row, dtype=jnp.int32)
    begins = ends - lengths_row
    first = jnp.take(begins, sequence[::block_rows]) // block_rows
    last = (jnp.take(ends, sequence[block_rows - 1 :: block_rows]) + block_rows - 1) // block_rows
    return jnp.stack([first, last])


def attention_forward_kernel(
    heads, rows, ranges, qkv_t, qkv, seq_col, seq_row, tiles, out, out_t, log_sums, keys
):
    span = qkv.shape[0]
    blocks = span // rows

    def stage(block, carry):
        at = pl.ds(pl.multiple_of(block * rows, rows), rows)
        for head in range(heads):
            keys[head, at, :] = qkv[at, head * 192 + 64 : head * 192 + 128]
        return carry

    lax.fori_loop(0, blocks, stage, 0)

    def query_block(block, carry):
        at = pl.ds(pl.multiple_of(block * rows, rows), rows)
        own_seq = seq_row[:, at]
        queries = [qkv_t[head * 192 : head * 192 + 64, at] for head in range(heads)]

        def key_block(other, state):
            there = pl.ds(pl.multiple_of(other * rows, rows), rows)
            same = seq_col[there, :] == own_seq
            kind = jnp.clip(other - block, -2, 2) + 2
            result = []
            for head in range(heads):
                top, total, acc = state[head]
                scores = jnp.dot(
                    keys[head, there, :], queries[head], preferred_element_type=jnp.float32
                )
                scores = jnp.where(same, scores + tiles[head, kind], NEG)
                top_now = jnp.maximum(top, jnp.max(scores, axis=0, keepdims=True))
                weights = jnp.exp(scores - top_now)
                shrink = jnp.exp(top - top_now)
                total = total * shrink + jnp.sum(weights, axis=0, keepdims=True)
                acc = acc * shrink + jnp.dot(
                    qkv_t[head * 192 + 128 : head * 192 + 192, there],
                    weights.astype(jnp.bfloat16),
                    preferred_element_type=jnp.float32,
                )
                result.append((top_now, total, acc))
            return tuple(result)

        initial = tuple(
            (
                jnp.full((1, rows), NEG, jnp.float32),
                jnp.zeros((1, rows), jnp.float32),
                jnp.zeros((64, rows), jnp.float32),
            )
            for head in range(heads)
        )
        state = lax.fori_loop(ranges[0, block], ranges[1, block], key_block, initial)
        for head in range(heads):
            top, total, acc = state[head]
            values = acc / total
            out_t[head * 64 : head * 64 + 64, at] = values
            log_sums[head, :, at] = top + jnp.log(total)
        joined = jnp.concatenate(
            [jnp.transpose(state[head][2] / state[head][1]) for head in range(heads)], axis=1
        )
        out[at, :] = joined.astype(jnp.bfloat16)
        return carry

    lax.fori_loop(0, blocks, query_block, 0)


def attention_backward_kernel(
    heads, rows, ranges, qkv_t, qkv, grad_t, grad, out_t, log_sums, seq_col, seq_row, tiles,
    grad_qkv, tile_sums, parts, grads, grad_q, grad_k, grad_v,
):
    span = qkv.shape[0]
    blocks = span // rows
    tile_sums[...] = jnp.zeros_like(tile_sums)
    grad_k[...] = jnp.zeros_like(grad_k)
    grad_v[...] = jnp.zeros_like(grad_v)

    def stage(block, carry):
        at = pl.ds(pl.multiple_of(block * rows, rows), rows)
        for head in range(heads):
            for kind in range(3):
                start = head * 192 + kind * 64
                parts[head, kind, at, :] = qkv[at, start : start + 64]
            grads[head, at, :] = grad[at, head * 64 : head * 64 + 64]
        return carry

    lax.fori_loop(0, blocks, stage, 0)

    def query_block(block, carry):
        at = pl.ds(pl.multiple_of(block * rows, rows), rows)
        own_seq = seq_row[:, at]
        inner = [
            jnp.sum(
                out_t[head * 64 : head * 64 + 64, at]
                * grad_t[head * 64 : head * 64 + 64, at].astype(jnp.float32),
                axis=0,
                keepdims=True,
            )
            for head in range(heads)
        ]
        grad_q[...] = jnp.zeros_like(grad_q)

        def key_block(other, state):
            there = pl.ds(pl.multiple_of(other * rows, rows), rows)
            same = seq_col[there, :] == own_seq
            kind = jnp.clip(other - block, -2, 2) + 2
            for head in range(heads):
                scores = jnp.dot(
                    parts[head, 1, there, :],
                    qkv_t[head * 192 : head * 192 + 64, at],
                    preferred_element_type=jnp.float32,
                )
                scores = jnp.where(same, scores + tiles[head, kind], NEG)
                probs = jnp.exp(scores - log_sums[head, :, at])
                grad_probs = jnp.dot(
                    parts[head, 2, there, :],
                    grad_t[head * 64 : head * 64 + 64, at],
                    preferred_element_type=jnp.float32,
                )
                grad_scores = probs * (grad_probs - inner[head])
                tile_sums[head, kind] += grad_scores
                low_scores = grad_scores.astype(jnp.bfloat16)
                grad_v[head, there, :] += jnp.dot(
                    probs.astype(jnp.bfloat16),
                    grads[head, at, :],
                    preferred_element_type=jnp.float32,
                )
                grad_k[head, there, :] += jnp.dot(
                    low_scores, parts[head, 0, at, :], preferred_element_type=jnp.float32
                )
                grad_q[head] += jnp.dot(
                    qkv_t[head * 192 + 64 : head * 192 + 128, there],
                    low_scores,
                    preferred_element_type=jnp.float32,
                )
            return state

        lax.fori_loop(ranges[0, block], ranges[1, block], key_block, 0)
        for head in range(heads):
            parts[head, 2 + 1, at, :] = (
                jnp.transpose(grad_q[head]) * HEAD ** (-0.5)
            ).astype(jnp.bfloat16)
        return carry

    lax.fori_loop(0, blocks, query_block, 0)

    def finish(block, carry):
        at = pl.ds(pl.multiple_of(block * rows, rows), rows)
        pieces = []
        for head in range(heads):
            pieces.append(parts[head, 3, at, :].astype(jnp.float32))
            pieces.append(grad_k[head, at, :])
            pieces.append(grad_v[head, at, :])
        grad_qkv[at, :] = jnp.concatenate(pieces, axis=1).astype(jnp.bfloat16)
        return carry

    lax.fori_loop(0, blocks, finish, 0)


def in_smem():
    return pl.BlockSpec(memory_space=pltpu.SMEM)


def in_vmem(count):
    return [pl.BlockSpec(memory_space=pltpu.VMEM)] * count


def attention_forward(ranges, qkv_t, qkv, sequence, tiles, heads, rows):
    span = qkv.shape[0]
    return pl.pallas_call(
        functools.partial(attention_forward_kernel, heads, rows),
        out_shape=(
            jax.ShapeDtypeStruct((span, heads * HEAD), jnp.bfloat16),
            jax.ShapeDtypeStruct((heads * HEAD, span), jnp.float32),
            jax.ShapeDtypeStruct((heads, 1, span), jnp.float32),
        ),
        in_specs=[in_smem()] + in_vmem(5),
        out_specs=tuple(in_vmem(3)),
        scratch_shapes=[pltpu.VMEM((heads, span, HEAD), jnp.bfloat16)],
        compiler_params=pltpu.CompilerParams(vmem_limit_bytes=48 * 2**20),
        cost_estimate=pl.CostEstimate(
            flops=4 * heads * span * span * HEAD,
            bytes_accessed=12 * 2**20,
            transcendentals=heads * span * span,
        ),
        name="attention_forward",
    )(ranges, qkv_t, qkv, sequence[:, None], sequence[None, :], tiles)


def attention_backward(
    ranges, qkv_t, qkv, grad_output, out_t, log_sums, sequence, tiles, heads, rows
):
    span = qkv.shape[0]
    return pl.pallas_call(
        functools.partial(attention_backward_kernel, heads, rows),
        out_shape=(
            jax.ShapeDtypeStruct((span, heads * 3 * HEAD), jnp.bfloat16),
            jax.ShapeDtypeStruct((heads, 5, rows, rows), jnp.float32),
        ),
        in_specs=[in_smem()] + in_vmem(9),
        out_specs=tuple(in_vmem(2)),
        scratch_shapes=[
            pltpu.VMEM((heads, 4, span, HEAD), jnp.bfloat16),
            pltpu.VMEM((heads, span, HEAD), jnp.bfloat16),
            pltpu.VMEM((heads, HEAD, rows), jnp.float32),
            pltpu.VMEM((heads, span, HEAD), jnp.float32),
            pltpu.VMEM((heads, span, HEAD), jnp.float32),
        ],
        compiler_params=pltpu.CompilerParams(vmem_limit_bytes=48 * 2**20),
        cost_estimate=pl.CostEstimate(
            flops=10 * heads * span * span * HEAD,
            bytes_accessed=20 * 2**20,
            transcendentals=heads * span * span,
        ),
        name="attention_backward",
    )(
        ranges,
        qkv_t,
        qkv,
        jnp.transpose(grad_output),
        grad_output,
        out_t,
        log_sums,
        sequence[:, None],
        sequence[None, :],
        tiles,
    )


def shards(
    x_in,
    grad_out,
    norm1_gain,
    qkv_weight,
    out_weight,
    bias_table,
    norm2_gain,
    router_weight,
    expert_in,
    expert_out,
    lengths,
    routes,
):
    tok_rows, model_width = x_in.shape
    heads_local = qkv_weight.shape[1] // (3 * HEAD)
    score_scale = HEAD ** (-0.5)
    tp_count = lax.axis_size("tp")
    dp_count = lax.axis_size("dp")
    normed_f, norm1_pull = jax.vjp(norm_apply, x_in, norm1_gain)
    normed_low = normed_f.astype(jnp.bfloat16)
    group_normed = gather_group(split_columns(normed_low))
    group_total = group_normed.shape[0]
    group_span = group_total // dp_count
    projected = sum_halves(row_product(group_normed, qkv_weight, False), group_span)
    kinds = jnp.arange(projected.shape[1], dtype=jnp.int32) // HEAD % 3
    qkv = (projected * jnp.where(kinds == 0, score_scale, 1.0)[None, :]).astype(jnp.bfloat16)
    qkv_t = jnp.transpose(qkv)
    sequence = segment_ids(lengths[0], group_span)
    head_start = lax.axis_index("tp") * heads_local
    table_heads = jnp.transpose(lax.dynamic_slice_in_dim(bias_table, head_start, heads_local, 1))
    block_rows = min(256, group_span)
    ranges = tile_ranges(lengths[0], sequence, block_rows)
    tiles = bias_tiles(table_heads, block_rows)
    attended, attended_t, log_sums = attention_forward(
        ranges, qkv_t, qkv, sequence, tiles, heads_local, block_rows
    )
    attended_group = gather_halves(attended)
    pair_rows = group_total // tp_count
    attn_cols = sum_blocks(row_product(attended_group, out_weight, False), pair_rows)
    hidden = x_in + join_rows(attn_cols)
    experts_count = lax.axis_size("ep")
    capacity = 2 * tok_rows // experts_count
    normed2_f, norm2_pull = jax.vjp(norm_apply, hidden, norm2_gain)
    normed2 = normed2_f.astype(jnp.bfloat16)
    logits = jnp.dot(normed2, router_weight, preferred_element_type=jnp.float32)
    shifted = jnp.exp(logits - jnp.max(logits, axis=1, keepdims=True))
    router = shifted / jnp.sum(shifted, axis=1, keepdims=True)
    route_int = (routes == jnp.arange(experts_count, dtype=jnp.int32)[None, :]).astype(jnp.int32)
    route_hot = route_int.astype(jnp.float32)
    gate = jnp.sum(router * route_hot, axis=1, keepdims=True)
    earlier = jnp.cumsum(route_int, axis=0) - route_int
    slot_index = jnp.sum(earlier * route_int, axis=1)
    position = routes[:, 0] * capacity + slot_index
    token_ids = jnp.arange(tok_rows, dtype=jnp.int32)
    slot_token = jnp.zeros((experts_count * capacity,), jnp.int32).at[position].set(token_ids)
    slot_live = jnp.zeros((experts_count * capacity, 1), jnp.bfloat16).at[position, 0].set(1.0)
    received = send_experts(jnp.take(normed2, slot_token, axis=0) * slot_live)
    full_in, full_out = (
        lax.all_gather(expert_in, ("tp", "dp"), axis=2, tiled=True),
        lax.all_gather(expert_out, ("tp", "dp"), axis=1, tiled=True),
    )
    pre_act = jnp.dot(received, full_in[0], preferred_element_type=jnp.float32)
    active_f, gelu_pull = jax.vjp(gelu_tanh, pre_act)
    active = active_f.astype(jnp.bfloat16)
    result_f = jnp.dot(active, full_out[0], preferred_element_type=jnp.float32)
    expert_tok = jnp.take(return_tokens(result_f.astype(jnp.bfloat16)), position, axis=0)
    out = hidden + gate * expert_tok.astype(jnp.float32)
    grad_result = (gate * grad_out).astype(jnp.bfloat16)
    grad_gate = jnp.sum(grad_out * expert_tok.astype(jnp.float32), axis=1, keepdims=True)
    grad_received = send_experts(jnp.take(grad_result, slot_token, axis=0) * slot_live)
    grad_active = contract_cols(grad_received, full_out[0])
    grad_pre = gelu_pull(grad_active)[0].astype(jnp.bfloat16)
    grad_first = contract_rows(active, grad_received)
    grad_second = contract_rows(grad_pre, received)
    stacked = lax.psum_scatter(
        jnp.concatenate([grad_first, grad_second], axis=1).astype(jnp.bfloat16),
        ("tp", "dp"),
        scatter_dimension=0,
        tiled=True,
    ).astype(jnp.float32)
    grad_weight_out = stacked[:, :model_width]
    grad_weight_in = jnp.transpose(stacked[:, model_width:])
    grad_sent = contract_cols(grad_pre, full_in[0])
    grad_expert_part = jnp.take(return_tokens(grad_sent.astype(jnp.bfloat16)), position, axis=0)
    grad_router_probs = grad_gate * route_hot
    grad_logits = (
        router * (grad_router_probs - jnp.sum(router * grad_router_probs, axis=1, keepdims=True))
    ).astype(jnp.bfloat16)
    grad_normed2 = grad_expert_part.astype(jnp.float32) + contract_cols(grad_logits, router_weight)
    grad_router = contract_rows(normed2, grad_logits)
    grad_hidden_norm, grad_gain_two = norm2_pull(grad_normed2)
    grad_hidden = grad_out + grad_hidden_norm
    grad_low = grad_hidden.astype(jnp.bfloat16)
    grad_attn_cols = gather_group(split_columns(grad_low))
    grad_out_weight = contract_rows(attended_group, grad_attn_cols)
    grad_attended = sum_halves(row_product(grad_attn_cols, out_weight, True), group_span)
    grad_qkv, tile_sums = attention_backward(
        ranges,
        qkv_t,
        qkv,
        grad_attended.astype(jnp.bfloat16),
        attended_t,
        log_sums,
        sequence,
        tiles,
        heads_local,
        block_rows,
    )
    grad_table_local = table_gradient(tile_sums, block_rows)
    grad_qkv_group = gather_halves(grad_qkv)
    grad_qkv_weight = contract_rows(group_normed, grad_qkv_group)
    grad_normed = join_rows(sum_blocks(row_product(grad_qkv_group, qkv_weight, True), pair_rows))
    grad_x_norm, grad_gain_one = norm1_pull(grad_normed)
    grad_in = grad_hidden + grad_x_norm
    table_full = lax.dynamic_update_slice(
        jnp.zeros(bias_table.shape, jnp.float32),
        jnp.transpose(grad_table_local),
        (jnp.int32(0), head_start),
    )
    grad_qkv_weight, grad_out_weight = (
        lax.psum(grad_qkv_weight.astype(jnp.bfloat16), "ep").astype(jnp.float32),
        lax.psum(grad_out_weight.astype(jnp.bfloat16), "ep").astype(jnp.float32),
    )
    grad_gain_one, grad_gain_two, grad_router, grad_table = lax.psum(
        (grad_gain_one, grad_gain_two, grad_router, table_full), ("ep", "tp", "dp")
    )
    return (
        out,
        grad_in,
        grad_gain_one,
        grad_qkv_weight,
        grad_out_weight,
        grad_table,
        grad_gain_two,
        grad_router,
        grad_weight_in[None],
        grad_weight_out[None],
    )


def solution(mesh):
    placed = (
        P(("ep", "tp", "dp"), None),
        P(("ep", "tp", "dp"), None),
        P(),
        P("dp", "tp"),
        P("tp", "dp"),
        P(),
        P(),
        P(),
        P("ep", None, ("tp", "dp")),
        P("ep", ("tp", "dp"), None),
        P(("ep", "dp"), None),
        P(("ep", "tp", "dp"), None),
    )
    return jax.shard_map(
        shards,
        mesh=mesh,
        in_specs=placed,
        out_specs=(
            P(("ep", "tp", "dp"), None),
            P(("ep", "tp", "dp"), None),
            P(),
            P("dp", "tp"),
            P("tp", "dp"),
            P(),
            P(),
            P(),
            P("ep", None, ("tp", "dp")),
            P("ep", ("tp", "dp"), None),
        ),
        check_vma=False,
    )
```

```python
import functools

import jax
import jax.numpy as jnp
from jax import lax
from jax.experimental import pallas as pl
from jax.experimental.pallas import tpu as pltpu
from jax.sharding import PartitionSpec as P

HEAD = 64


EPS = 1e-06
NEG = -1e30
STEP_EDGES = (1, 2, 3, 4, 5, 6, 7, 8, 12, 16, 23, 32, 46, 64, 91)
GELU_C = 0.7978845608028654


def segment_ids(lengths_row, row_count):
    seq_ends = jnp.cumsum(lengths_row, dtype=jnp.int32)
    positions = jnp.arange(row_count, dtype=jnp.int32)
    return jnp.sum(
        (positions[:, None] >= seq_ends[None, :-1]).astype(jnp.int32), axis=1, dtype=jnp.int32
    )


def gelu_tanh(inputs):
    return 0.5 * inputs * (1.0 + jnp.tanh(GELU_C * (inputs + 0.044715 * inputs * inputs * inputs)))


def norm_apply(values, gain_vector):
    return values * lax.rsqrt(jnp.mean(values * values, axis=-1, keepdims=True) + EPS) * gain_vector


def contract_rows(left, right):
    return lax.dot_general(
        left, right, (((0,), (0,)), ((), ())), preferred_element_type=jnp.float32
    )


def contract_cols(left, right):
    return lax.dot_general(
        left, right, (((1,), (1,)), ((), ())), preferred_element_type=jnp.float32
    )


def row_product(left, right, transposed):

    def product(row_start, row_count):
        if transposed:
            return contract_cols(left, right)
        return jnp.dot(left, right, preferred_element_type=jnp.float32)

    return product


def split_columns(values):
    return lax.all_to_all(values, "dp", split_axis=1, concat_axis=0, tiled=True)


def gather_group(values):
    return lax.all_gather(values, "tp", axis=0, tiled=True)


def sum_halves(product, row_count):
    return lax.psum_scatter(
        product(jnp.int32(0), row_count * lax.axis_size("dp")),
        "dp",
        scatter_dimension=0,
        tiled=True,
    )


def gather_halves(values):
    return lax.all_gather(values, "dp", axis=0, tiled=True)


def sum_blocks(product, row_count):
    return lax.psum_scatter(
        product(jnp.int32(0), lax.axis_size("tp") * row_count).astype(jnp.bfloat16),
        "tp",
        scatter_dimension=0,
        tiled=True,
    ).astype(jnp.float32)


def join_rows(values):
    return lax.all_to_all(
        values.astype(jnp.bfloat16), "dp", split_axis=0, concat_axis=1, tiled=True
    ).astype(values.dtype)


def send_experts(values):
    return lax.all_to_all(values, "ep", split_axis=0, concat_axis=0, tiled=True)


def return_tokens(values):
    return lax.all_to_all(values, "ep", split_axis=0, concat_axis=0, tiled=True)


def rel_bucket(offsets):
    distance = jnp.abs(offsets)
    bucket = jnp.where(offsets > 0, 16, 0)
    for edge in STEP_EDGES:
        bucket = bucket + (distance >= edge).astype(jnp.int32)
    return bucket


def tile_offsets(block_rows):
    keys = jnp.arange(3 * block_rows, dtype=jnp.int32)[:, None] - block_rows
    return keys - jnp.arange(block_rows, dtype=jnp.int32)[None, :]


def bias_tiles(table_heads, block_rows):
    offsets = tile_offsets(block_rows)[None]
    distance = jnp.abs(offsets)
    ahead = offsets > 0
    near = jnp.zeros((1, 1, 1), jnp.float32) + table_heads[:, 0][:, None, None]
    for index, edge in enumerate(STEP_EDGES):
        step = jnp.where(
            ahead,
            table_heads[:, 17 + index][:, None, None],
            table_heads[:, 1 + index][:, None, None],
        )
        near = jnp.where(distance >= edge, step, near)
    heads = table_heads.shape[0]
    flat = jnp.ones((1, block_rows, block_rows), jnp.float32)
    return jnp.concatenate(
        [
            table_heads[:, 15][:, None, None] * flat,
            near,
            table_heads[:, 31][:, None, None] * flat,
        ],
        axis=1,
    ).reshape(heads, 5, block_rows, block_rows)


def table_gradient(tile_sums, block_rows):
    heads = tile_sums.shape[0]
    near = tile_sums[:, 1:4].reshape(heads, 3 * block_rows, block_rows)
    buckets = rel_bucket(tile_offsets(block_rows))
    sums = [
        jnp.sum(jnp.where(buckets[None] == index, near, 0.0), axis=(1, 2))
        for index in range(32)
    ]
    sums[15] = sums[15] + jnp.sum(tile_sums[:, 0], axis=(1, 2))
    sums[31] = sums[31] + jnp.sum(tile_sums[:, 4], axis=(1, 2))
    return jnp.stack(sums, axis=1)


def tile_ranges(lengths_row, sequence, block_rows):
    ends = jnp.cumsum(lengths_row, dtype=jnp.int32)
    begins = ends - lengths_row
    first = jnp.take(begins, sequence[::block_rows]) // block_rows
    last = (jnp.take(ends, sequence[block_rows - 1 :: block_rows]) + block_rows - 1) // block_rows
    return jnp.stack([first, last])


def attention_forward_kernel(
    heads, rows, ranges, qkv_t, qkv, seq_col, seq_row, tiles, out, out_t, log_sums, keys
):
    span = qkv.shape[0]
    blocks = span // rows

    def stage(block, carry):
        at = pl.ds(pl.multiple_of(block * rows, rows), rows)
        for head in range(heads):
            keys[head, at, :] = qkv[at, head * 192 + 64 : head * 192 + 128]
        return carry

    lax.fori_loop(0, blocks, stage, 0)

    def query_block(block, carry):
        at = pl.ds(pl.multiple_of(block * rows, rows), rows)
        own_seq = seq_row[:, at]
        queries = [qkv_t[head * 192 : head * 192 + 64, at] for head in range(heads)]

        def key_block(other, state):
            there = pl.ds(pl.multiple_of(other * rows, rows), rows)
            same = seq_col[there, :] == own_seq
            kind = jnp.clip(other - block, -2, 2) + 2
            result = []
            for head in range(heads):
                top, total, acc = state[head]
                scores = jnp.dot(
                    keys[head, there, :], queries[head], preferred_element_type=jnp.float32
                )
                scores = jnp.where(same, scores + tiles[head, kind], NEG)
                top_now = jnp.maximum(top, jnp.max(scores, axis=0, keepdims=True))
                weights = jnp.exp(scores - top_now)
                shrink = jnp.exp(top - top_now)
                total = total * shrink + jnp.sum(weights, axis=0, keepdims=True)
                acc = acc * shrink + jnp.dot(
                    qkv_t[head * 192 + 128 : head * 192 + 192, there],
                    weights.astype(jnp.bfloat16),
                    preferred_element_type=jnp.float32,
                )
                result.append((top_now, total, acc))
            return tuple(result)

        initial = tuple(
            (
                jnp.full((1, rows), NEG, jnp.float32),
                jnp.zeros((1, rows), jnp.float32),
                jnp.zeros((64, rows), jnp.float32),
            )
            for head in range(heads)
        )
        state = lax.fori_loop(ranges[0, block], ranges[1, block], key_block, initial)
        for head in range(heads):
            top, total, acc = state[head]
            values = acc / total
            out_t[head * 64 : head * 64 + 64, at] = values
            log_sums[head, :, at] = top + jnp.log(total)
        joined = jnp.concatenate(
            [jnp.transpose(state[head][2] / state[head][1]) for head in range(heads)], axis=1
        )
        out[at, :] = joined.astype(jnp.bfloat16)
        return carry

    lax.fori_loop(0, blocks, query_block, 0)


def attention_backward_kernel(
    heads, rows, ranges, qkv_t, qkv, grad_t, grad, out_t, log_sums, seq_col, seq_row, tiles,
    grad_qkv, tile_sums, parts, grads, grad_q, grad_k, grad_v,
):
    span = qkv.shape[0]
    blocks = span // rows
    tile_sums[...] = jnp.zeros_like(tile_sums)
    grad_k[...] = jnp.zeros_like(grad_k)
    grad_v[...] = jnp.zeros_like(grad_v)

    def stage(block, carry):
        at = pl.ds(pl.multiple_of(block * rows, rows), rows)
        for head in range(heads):
            for kind in range(3):
                start = head * 192 + kind * 64
                parts[head, kind, at, :] = qkv[at, start : start + 64]
            grads[head, at, :] = grad[at, head * 64 : head * 64 + 64]
        return carry

    lax.fori_loop(0, blocks, stage, 0)

    def query_block(block, carry):
        at = pl.ds(pl.multiple_of(block * rows, rows), rows)
        own_seq = seq_row[:, at]
        inner = [
            jnp.sum(
                out_t[head * 64 : head * 64 + 64, at]
                * grad_t[head * 64 : head * 64 + 64, at].astype(jnp.float32),
                axis=0,
                keepdims=True,
            )
            for head in range(heads)
        ]
        grad_q[...] = jnp.zeros_like(grad_q)

        def key_block(other, state):
            there = pl.ds(pl.multiple_of(other * rows, rows), rows)
            same = seq_col[there, :] == own_seq
            kind = jnp.clip(other - block, -2, 2) + 2
            for head in range(heads):
                scores = jnp.dot(
                    parts[head, 1, there, :],
                    qkv_t[head * 192 : head * 192 + 64, at],
                    preferred_element_type=jnp.float32,
                )
                scores = jnp.where(same, scores + tiles[head, kind], NEG)
                probs = jnp.exp(scores - log_sums[head, :, at])
                grad_probs = jnp.dot(
                    parts[head, 2, there, :],
                    grad_t[head * 64 : head * 64 + 64, at],
                    preferred_element_type=jnp.float32,
                )
                grad_scores = probs * (grad_probs - inner[head])
                tile_sums[head, kind] += grad_scores
                low_scores = grad_scores.astype(jnp.bfloat16)
                grad_v[head, there, :] += jnp.dot(
                    probs.astype(jnp.bfloat16),
                    grads[head, at, :],
                    preferred_element_type=jnp.float32,
                )
                grad_k[head, there, :] += jnp.dot(
                    low_scores, parts[head, 0, at, :], preferred_element_type=jnp.float32
                )
                grad_q[head] += jnp.dot(
                    qkv_t[head * 192 + 64 : head * 192 + 128, there],
                    low_scores,
                    preferred_element_type=jnp.float32,
                )
            return state

        lax.fori_loop(ranges[0, block], ranges[1, block], key_block, 0)
        for head in range(heads):
            parts[head, 2 + 1, at, :] = (
                jnp.transpose(grad_q[head]) * HEAD ** (-0.5)
            ).astype(jnp.bfloat16)
        return carry

    lax.fori_loop(0, blocks, query_block, 0)

    def finish(block, carry):
        at = pl.ds(pl.multiple_of(block * rows, rows), rows)
        pieces = []
        for head in range(heads):
            pieces.append(parts[head, 3, at, :].astype(jnp.float32))
            pieces.append(grad_k[head, at, :])
            pieces.append(grad_v[head, at, :])
        grad_qkv[at, :] = jnp.concatenate(pieces, axis=1).astype(jnp.bfloat16)
        return carry

    lax.fori_loop(0, blocks, finish, 0)


def in_smem():
    return pl.BlockSpec(memory_space=pltpu.SMEM)


def in_vmem(count):
    return [pl.BlockSpec(memory_space=pltpu.VMEM)] * count


def attention_forward(ranges, qkv_t, qkv, sequence, tiles, heads, rows):
    span = qkv.shape[0]
    return pl.pallas_call(
        functools.partial(attention_forward_kernel, heads, rows),
        out_shape=(
            jax.ShapeDtypeStruct((span, heads * HEAD), jnp.bfloat16),
            jax.ShapeDtypeStruct((heads * HEAD, span), jnp.float32),
            jax.ShapeDtypeStruct((heads, 1, span), jnp.float32),
        ),
        in_specs=[in_smem()] + in_vmem(5),
        out_specs=tuple(in_vmem(3)),
        scratch_shapes=[pltpu.VMEM((heads, span, HEAD), jnp.bfloat16)],
        compiler_params=pltpu.CompilerParams(vmem_limit_bytes=48 * 2**20),
        cost_estimate=pl.CostEstimate(
            flops=4 * heads * span * span * HEAD,
            bytes_accessed=12 * 2**20,
            transcendentals=heads * span * span,
        ),
        name="attention_forward",
    )(ranges, qkv_t, qkv, sequence[:, None], sequence[None, :], tiles)


def attention_backward(
    ranges, qkv_t, qkv, grad_output, out_t, log_sums, sequence, tiles, heads, rows
):
    span = qkv.shape[0]
    return pl.pallas_call(
        functools.partial(attention_backward_kernel, heads, rows),
        out_shape=(
            jax.ShapeDtypeStruct((span, heads * 3 * HEAD), jnp.bfloat16),
            jax.ShapeDtypeStruct((heads, 5, rows, rows), jnp.float32),
        ),
        in_specs=[in_smem()] + in_vmem(9),
        out_specs=tuple(in_vmem(2)),
        scratch_shapes=[
            pltpu.VMEM((heads, 4, span, HEAD), jnp.bfloat16),
            pltpu.VMEM((heads, span, HEAD), jnp.bfloat16),
            pltpu.VMEM((heads, HEAD, rows), jnp.float32),
            pltpu.VMEM((heads, span, HEAD), jnp.float32),
            pltpu.VMEM((heads, span, HEAD), jnp.float32),
        ],
        compiler_params=pltpu.CompilerParams(vmem_limit_bytes=48 * 2**20),
        cost_estimate=pl.CostEstimate(
            flops=10 * heads * span * span * HEAD,
            bytes_accessed=20 * 2**20,
            transcendentals=heads * span * span,
        ),
        name="attention_backward",
    )(
        ranges,
        qkv_t,
        qkv,
        jnp.transpose(grad_output),
        grad_output,
        out_t,
        log_sums,
        sequence[:, None],
        sequence[None, :],
        tiles,
    )


def shards(
    x_in,
    grad_out,
    norm1_gain,
    qkv_weight,
    out_weight,
    bias_table,
    norm2_gain,
    router_weight,
    expert_in,
    expert_out,
    lengths,
    routes,
):
    tok_rows, model_width = x_in.shape
    heads_local = qkv_weight.shape[1] // (3 * HEAD)
    score_scale = HEAD ** (-0.5)
    tp_count = lax.axis_size("tp")
    dp_count = lax.axis_size("dp")
    normed_f, norm1_pull = jax.vjp(norm_apply, x_in, norm1_gain)
    normed_low = normed_f.astype(jnp.bfloat16)
    group_normed = gather_group(split_columns(normed_low))
    group_total = group_normed.shape[0]
    group_span = group_total // dp_count
    projected = sum_halves(row_product(group_normed, qkv_weight, False), group_span)
    kinds = jnp.arange(projected.shape[1], dtype=jnp.int32) // HEAD % 3
    qkv = (projected * jnp.where(kinds == 0, score_scale, 1.0)[None, :]).astype(jnp.bfloat16)
    qkv_t = jnp.transpose(qkv)
    sequence = segment_ids(lengths[0], group_span)
    head_start = lax.axis_index("tp") * heads_local
    table_heads = jnp.transpose(lax.dynamic_slice_in_dim(bias_table, head_start, heads_local, 1))
    block_rows = min(256, group_span)
    ranges = tile_ranges(lengths[0], sequence, block_rows)
    tiles = bias_tiles(table_heads, block_rows)
    attended, attended_t, log_sums = attention_forward(
        ranges, qkv_t, qkv, sequence, tiles, heads_local, block_rows
    )
    attended_group = gather_halves(attended)
    pair_rows = group_total // tp_count
    attn_cols = sum_blocks(row_product(attended_group, out_weight, False), pair_rows)
    hidden = x_in + join_rows(attn_cols)
    experts_count = lax.axis_size("ep")
    capacity = 2 * tok_rows // experts_count
    normed2_f, norm2_pull = jax.vjp(norm_apply, hidden, norm2_gain)
    normed2 = normed2_f.astype(jnp.bfloat16)
    logits = jnp.dot(normed2, router_weight, preferred_element_type=jnp.float32)
    shifted = jnp.exp(logits - jnp.max(logits, axis=1, keepdims=True))
    router = shifted / jnp.sum(shifted, axis=1, keepdims=True)
    route_int = (routes == jnp.arange(experts_count, dtype=jnp.int32)[None, :]).astype(jnp.int32)
    route_hot = route_int.astype(jnp.float32)
    gate = jnp.sum(router * route_hot, axis=1, keepdims=True)
    earlier = jnp.cumsum(route_int, axis=0) - route_int
    slot_index = jnp.sum(earlier * route_int, axis=1)
    position = routes[:, 0] * capacity + slot_index
    token_ids = jnp.arange(tok_rows, dtype=jnp.int32)
    slot_token = jnp.zeros((experts_count * capacity,), jnp.int32).at[position].set(token_ids)
    slot_live = jnp.zeros((experts_count * capacity, 1), jnp.bfloat16).at[position, 0].set(1.0)
    received = send_experts(jnp.take(normed2, slot_token, axis=0) * slot_live)
    full_in, full_out = (
        lax.all_gather(expert_in, ("tp", "dp"), axis=2, tiled=True),
        lax.all_gather(expert_out, ("tp", "dp"), axis=1, tiled=True),
    )
    pre_act = jnp.dot(received, full_in[0], preferred_element_type=jnp.float32)
    active_f, gelu_pull = jax.vjp(gelu_tanh, pre_act)
    active = active_f.astype(jnp.bfloat16)
    result_f = jnp.dot(active, full_out[0], preferred_element_type=jnp.float32)
    expert_tok = jnp.take(return_tokens(result_f.astype(jnp.bfloat16)), position, axis=0)
    out = hidden + gate * expert_tok.astype(jnp.float32)
    grad_result = (gate * grad_out).astype(jnp.bfloat16)
    grad_gate = jnp.sum(grad_out * expert_tok.astype(jnp.float32), axis=1, keepdims=True)
    grad_received = send_experts(jnp.take(grad_result, slot_token, axis=0) * slot_live)
    grad_active = contract_cols(grad_received, full_out[0])
    grad_pre = gelu_pull(grad_active)[0].astype(jnp.bfloat16)
    grad_first = contract_rows(active, grad_received)
    grad_second = contract_rows(grad_pre, received)
    stacked_in = jnp.concatenate([grad_first, grad_second], axis=1).astype(jnp.bfloat16)
    grad_sent = contract_cols(grad_pre, full_in[0])
    grad_expert_part = jnp.take(return_tokens(grad_sent.astype(jnp.bfloat16)), position, axis=0)
    grad_router_probs = grad_gate * route_hot
    grad_logits = (
        router * (grad_router_probs - jnp.sum(router * grad_router_probs, axis=1, keepdims=True))
    ).astype(jnp.bfloat16)
    grad_normed2 = grad_expert_part.astype(jnp.float32) + contract_cols(grad_logits, router_weight)
    grad_router = contract_rows(normed2, grad_logits)
    grad_hidden_norm, grad_gain_two = norm2_pull(grad_normed2)
    grad_hidden = grad_out + grad_hidden_norm
    grad_low = grad_hidden.astype(jnp.bfloat16)
    grad_attn_cols = gather_group(split_columns(grad_low))
    grad_out_weight = contract_rows(attended_group, grad_attn_cols)
    grad_attended = sum_halves(row_product(grad_attn_cols, out_weight, True), group_span)
    grad_attended, stacked_in = lax.optimization_barrier(
        (grad_attended.astype(jnp.bfloat16), stacked_in)
    )
    stacked = lax.psum_scatter(stacked_in, ("tp", "dp"), scatter_dimension=0, tiled=True)
    grad_qkv, tile_sums = attention_backward(
        ranges,
        qkv_t,
        qkv,
        grad_attended,
        attended_t,
        log_sums,
        sequence,
        tiles,
        heads_local,
        block_rows,
    )
    grad_table_local = table_gradient(tile_sums, block_rows)
    grad_qkv, stacked = lax.optimization_barrier((grad_qkv, stacked))
    stacked = stacked.astype(jnp.float32)
    grad_weight_out = stacked[:, :model_width]
    grad_weight_in = jnp.transpose(stacked[:, model_width:])
    grad_qkv_group = gather_halves(grad_qkv)
    grad_qkv_weight = contract_rows(group_normed, grad_qkv_group)
    grad_normed = join_rows(sum_blocks(row_product(grad_qkv_group, qkv_weight, True), pair_rows))
    grad_x_norm, _ = norm1_pull(grad_normed)
    gain_part = jnp.sum(grad_qkv_weight * qkv_weight.astype(jnp.float32), axis=1)
    grad_gain_one = (
        lax.dynamic_update_slice(
            jnp.zeros((model_width,), jnp.float32),
            gain_part,
            (lax.axis_index("dp") * gain_part.shape[0],),
        )
        / norm1_gain
    )
    grad_in = grad_hidden + grad_x_norm
    table_full = lax.dynamic_update_slice(
        jnp.zeros(bias_table.shape, jnp.float32),
        jnp.transpose(grad_table_local),
        (jnp.int32(0), head_start),
    )
    grad_qkv_weight, grad_out_weight = (
        lax.psum(grad_qkv_weight.astype(jnp.bfloat16), "ep").astype(jnp.float32),
        lax.psum(grad_out_weight.astype(jnp.bfloat16), "ep").astype(jnp.float32),
    )
    grad_gain_one, grad_gain_two, grad_router, grad_table = lax.psum(
        (grad_gain_one, grad_gain_two, grad_router, table_full), ("ep", "tp", "dp")
    )
    return (
        out,
        grad_in,
        grad_gain_one,
        grad_qkv_weight,
        grad_out_weight,
        grad_table,
        grad_gain_two,
        grad_router,
        grad_weight_in[None],
        grad_weight_out[None],
    )


def solution(mesh):
    placed = (
        P(("ep", "tp", "dp"), None),
        P(("ep", "tp", "dp"), None),
        P(),
        P("dp", "tp"),
        P("tp", "dp"),
        P(),
        P(),
        P(),
        P("ep", None, ("tp", "dp")),
        P("ep", ("tp", "dp"), None),
        P(("ep", "dp"), None),
        P(("ep", "tp", "dp"), None),
    )
    return jax.shard_map(
        shards,
        mesh=mesh,
        in_specs=placed,
        out_specs=(
            P(("ep", "tp", "dp"), None),
            P(("ep", "tp", "dp"), None),
            P(),
            P("dp", "tp"),
            P("tp", "dp"),
            P(),
            P(),
            P(),
            P("ep", None, ("tp", "dp")),
            P("ep", ("tp", "dp"), None),
        ),
        check_vma=False,
    )
```

```python
import functools

import jax
import jax.numpy as jnp
from jax import lax
from jax.experimental import pallas as pl
from jax.experimental.pallas import tpu as pltpu
from jax.sharding import PartitionSpec as P

HEAD = 64


EPS = 1e-06
NEG = -1e30
STEP_EDGES = (1, 2, 3, 4, 5, 6, 7, 8, 12, 16, 23, 32, 46, 64, 91)
GELU_C = 0.7978845608028654


def segment_ids(lengths_row, row_count):
    seq_ends = jnp.cumsum(lengths_row, dtype=jnp.int32)
    positions = jnp.arange(row_count, dtype=jnp.int32)
    return jnp.sum(
        (positions[:, None] >= seq_ends[None, :-1]).astype(jnp.int32), axis=1, dtype=jnp.int32
    )


def gelu_tanh(inputs):
    return 0.5 * inputs * (1.0 + jnp.tanh(GELU_C * (inputs + 0.044715 * inputs * inputs * inputs)))


def norm_apply(values, gain_vector):
    return values * lax.rsqrt(jnp.mean(values * values, axis=-1, keepdims=True) + EPS) * gain_vector


def contract_rows(left, right):
    return lax.dot_general(
        left, right, (((0,), (0,)), ((), ())), preferred_element_type=jnp.float32
    )


def contract_cols(left, right):
    return lax.dot_general(
        left, right, (((1,), (1,)), ((), ())), preferred_element_type=jnp.float32
    )


def row_product(left, right, transposed):

    def product(row_start, row_count):
        if transposed:
            return contract_cols(left, right)
        return jnp.dot(left, right, preferred_element_type=jnp.float32)

    return product


def split_columns(values):
    return lax.all_to_all(values, "dp", split_axis=1, concat_axis=0, tiled=True)


def gather_group(values):
    return lax.all_gather(values, "tp", axis=0, tiled=True)


def sum_halves(product, row_count):
    return lax.psum_scatter(
        product(jnp.int32(0), row_count * lax.axis_size("dp")),
        "dp",
        scatter_dimension=0,
        tiled=True,
    )


def gather_halves(values):
    return lax.all_gather(values, "dp", axis=0, tiled=True)


def sum_blocks(product, row_count):
    return lax.psum_scatter(
        product(jnp.int32(0), lax.axis_size("tp") * row_count).astype(jnp.bfloat16),
        "tp",
        scatter_dimension=0,
        tiled=True,
    ).astype(jnp.float32)


def join_rows(values):
    return lax.all_to_all(
        values.astype(jnp.bfloat16), "dp", split_axis=0, concat_axis=1, tiled=True
    ).astype(values.dtype)


def send_experts(values):
    return lax.all_to_all(values, "ep", split_axis=0, concat_axis=0, tiled=True)


def return_tokens(values):
    return lax.all_to_all(values, "ep", split_axis=0, concat_axis=0, tiled=True)


def rel_bucket(offsets):
    distance = jnp.abs(offsets)
    bucket = jnp.where(offsets > 0, 16, 0)
    for edge in STEP_EDGES:
        bucket = bucket + (distance >= edge).astype(jnp.int32)
    return bucket


def tile_offsets(block_rows):
    keys = jnp.arange(3 * block_rows, dtype=jnp.int32)[:, None] - block_rows
    return keys - jnp.arange(block_rows, dtype=jnp.int32)[None, :]


def bias_tiles(table_heads, block_rows):
    offsets = tile_offsets(block_rows)[None]
    distance = jnp.abs(offsets)
    ahead = offsets > 0
    near = jnp.zeros((1, 1, 1), jnp.float32) + table_heads[:, 0][:, None, None]
    for index, edge in enumerate(STEP_EDGES):
        step = jnp.where(
            ahead,
            table_heads[:, 17 + index][:, None, None],
            table_heads[:, 1 + index][:, None, None],
        )
        near = jnp.where(distance >= edge, step, near)
    heads = table_heads.shape[0]
    flat = jnp.ones((1, block_rows, block_rows), jnp.float32)
    return jnp.concatenate(
        [
            table_heads[:, 15][:, None, None] * flat,
            near,
            table_heads[:, 31][:, None, None] * flat,
        ],
        axis=1,
    ).reshape(heads, 5, block_rows, block_rows)


def table_gradient(tile_sums, block_rows):
    heads = tile_sums.shape[0]
    near = tile_sums[:, 1:4].reshape(heads, 3 * block_rows, block_rows)
    buckets = rel_bucket(tile_offsets(block_rows))
    sums = [
        jnp.sum(jnp.where(buckets[None] == index, near, 0.0), axis=(1, 2))
        for index in range(32)
    ]
    sums[15] = sums[15] + jnp.sum(tile_sums[:, 0], axis=(1, 2))
    sums[31] = sums[31] + jnp.sum(tile_sums[:, 4], axis=(1, 2))
    return jnp.stack(sums, axis=1)


def tile_ranges(lengths_row, sequence, block_rows):
    ends = jnp.cumsum(lengths_row, dtype=jnp.int32)
    begins = ends - lengths_row
    first = jnp.take(begins, sequence[::block_rows]) // block_rows
    last = (jnp.take(ends, sequence[block_rows - 1 :: block_rows]) + block_rows - 1) // block_rows
    return jnp.stack([first, last])


def attention_forward_kernel(
    heads, rows, ranges, qkv_t, qkv, seq_col, seq_row, tiles, out, out_t, log_sums, keys
):
    span = qkv.shape[0]
    blocks = span // rows

    def stage(block, carry):
        at = pl.ds(pl.multiple_of(block * rows, rows), rows)
        for head in range(heads):
            keys[head, at, :] = qkv[at, head * 192 + 64 : head * 192 + 128]
        return carry

    lax.fori_loop(0, blocks, stage, 0)

    def query_block(block, carry):
        at = pl.ds(pl.multiple_of(block * rows, rows), rows)
        own_seq = seq_row[:, at]
        queries = [qkv_t[head * 192 : head * 192 + 64, at] for head in range(heads)]

        def key_block(other, state):
            there = pl.ds(pl.multiple_of(other * rows, rows), rows)
            same = seq_col[there, :] == own_seq
            kind = jnp.clip(other - block, -2, 2) + 2
            result = []
            for head in range(heads):
                top, total, acc = state[head]
                scores = jnp.dot(
                    keys[head, there, :], queries[head], preferred_element_type=jnp.float32
                )
                scores = jnp.where(same, scores + tiles[head, kind], NEG)
                top_now = jnp.maximum(top, jnp.max(scores, axis=0, keepdims=True))
                weights = jnp.exp(scores - top_now)
                shrink = jnp.exp(top - top_now)
                total = total * shrink + jnp.sum(weights, axis=0, keepdims=True)
                acc = acc * shrink + jnp.dot(
                    qkv_t[head * 192 + 128 : head * 192 + 192, there],
                    weights.astype(jnp.bfloat16),
                    preferred_element_type=jnp.float32,
                )
                result.append((top_now, total, acc))
            return tuple(result)

        initial = tuple(
            (
                jnp.full((1, rows), NEG, jnp.float32),
                jnp.zeros((1, rows), jnp.float32),
                jnp.zeros((64, rows), jnp.float32),
            )
            for head in range(heads)
        )
        state = lax.fori_loop(ranges[0, block], ranges[1, block], key_block, initial)
        for head in range(heads):
            top, total, acc = state[head]
            values = acc / total
            out_t[head * 64 : head * 64 + 64, at] = values
            log_sums[head, :, at] = top + jnp.log(total)
        joined = jnp.concatenate(
            [jnp.transpose(state[head][2] / state[head][1]) for head in range(heads)], axis=1
        )
        out[at, :] = joined.astype(jnp.bfloat16)
        return carry

    lax.fori_loop(0, blocks, query_block, 0)


def attention_backward_kernel(
    heads, rows, ranges, qkv_t, qkv, grad_t, grad, out_t, log_sums, seq_col, seq_row, tiles,
    grad_qkv, tile_sums, parts, grads, grad_q, grad_k, grad_v,
):
    span = qkv.shape[0]
    blocks = span // rows
    tile_sums[...] = jnp.zeros_like(tile_sums)
    grad_k[...] = jnp.zeros_like(grad_k)
    grad_v[...] = jnp.zeros_like(grad_v)

    def stage(block, carry):
        at = pl.ds(pl.multiple_of(block * rows, rows), rows)
        for head in range(heads):
            for kind in range(3):
                start = head * 192 + kind * 64
                parts[head, kind, at, :] = qkv[at, start : start + 64]
            grads[head, at, :] = grad[at, head * 64 : head * 64 + 64]
        return carry

    lax.fori_loop(0, blocks, stage, 0)

    def query_block(block, carry):
        at = pl.ds(pl.multiple_of(block * rows, rows), rows)
        own_seq = seq_row[:, at]
        inner = [
            jnp.sum(
                out_t[head * 64 : head * 64 + 64, at]
                * grad_t[head * 64 : head * 64 + 64, at].astype(jnp.float32),
                axis=0,
                keepdims=True,
            )
            for head in range(heads)
        ]
        grad_q[...] = jnp.zeros_like(grad_q)

        def key_block(other, state):
            there = pl.ds(pl.multiple_of(other * rows, rows), rows)
            same = seq_col[there, :] == own_seq
            kind = jnp.clip(other - block, -2, 2) + 2
            for head in range(heads):
                scores = jnp.dot(
                    parts[head, 1, there, :],
                    qkv_t[head * 192 : head * 192 + 64, at],
                    preferred_element_type=jnp.float32,
                )
                scores = jnp.where(same, scores + tiles[head, kind], NEG)
                probs = jnp.exp(scores - log_sums[head, :, at])
                grad_probs = jnp.dot(
                    parts[head, 2, there, :],
                    grad_t[head * 64 : head * 64 + 64, at],
                    preferred_element_type=jnp.float32,
                )
                grad_scores = probs * (grad_probs - inner[head])
                tile_sums[head, kind] += grad_scores
                low_scores = grad_scores.astype(jnp.bfloat16)
                grad_v[head, there, :] += jnp.dot(
                    probs.astype(jnp.bfloat16),
                    grads[head, at, :],
                    preferred_element_type=jnp.float32,
                )
                grad_k[head, there, :] += jnp.dot(
                    low_scores, parts[head, 0, at, :], preferred_element_type=jnp.float32
                )
                grad_q[head] += jnp.dot(
                    qkv_t[head * 192 + 64 : head * 192 + 128, there],
                    low_scores,
                    preferred_element_type=jnp.float32,
                )
            return state

        lax.fori_loop(ranges[0, block], ranges[1, block], key_block, 0)
        for head in range(heads):
            parts[head, 2 + 1, at, :] = (
                jnp.transpose(grad_q[head]) * HEAD ** (-0.5)
            ).astype(jnp.bfloat16)
        return carry

    lax.fori_loop(0, blocks, query_block, 0)

    def finish(block, carry):
        at = pl.ds(pl.multiple_of(block * rows, rows), rows)
        pieces = []
        for head in range(heads):
            pieces.append(parts[head, 3, at, :].astype(jnp.float32))
            pieces.append(grad_k[head, at, :])
            pieces.append(grad_v[head, at, :])
        grad_qkv[at, :] = jnp.concatenate(pieces, axis=1).astype(jnp.bfloat16)
        return carry

    lax.fori_loop(0, blocks, finish, 0)


def in_smem():
    return pl.BlockSpec(memory_space=pltpu.SMEM)


def in_vmem(count):
    return [pl.BlockSpec(memory_space=pltpu.VMEM)] * count


def attention_forward(ranges, qkv_t, qkv, sequence, tiles, heads, rows):
    span = qkv.shape[0]
    return pl.pallas_call(
        functools.partial(attention_forward_kernel, heads, rows),
        out_shape=(
            jax.ShapeDtypeStruct((span, heads * HEAD), jnp.bfloat16),
            jax.ShapeDtypeStruct((heads * HEAD, span), jnp.float32),
            jax.ShapeDtypeStruct((heads, 1, span), jnp.float32),
        ),
        in_specs=[in_smem()] + in_vmem(5),
        out_specs=tuple(in_vmem(3)),
        scratch_shapes=[pltpu.VMEM((heads, span, HEAD), jnp.bfloat16)],
        compiler_params=pltpu.CompilerParams(vmem_limit_bytes=48 * 2**20),
        cost_estimate=pl.CostEstimate(
            flops=4 * heads * span * span * HEAD,
            bytes_accessed=12 * 2**20,
            transcendentals=heads * span * span,
        ),
        name="attention_forward",
    )(ranges, qkv_t, qkv, sequence[:, None], sequence[None, :], tiles)


def attention_backward(
    ranges, qkv_t, qkv, grad_output, out_t, log_sums, sequence, tiles, heads, rows
):
    span = qkv.shape[0]
    return pl.pallas_call(
        functools.partial(attention_backward_kernel, heads, rows),
        out_shape=(
            jax.ShapeDtypeStruct((span, heads * 3 * HEAD), jnp.bfloat16),
            jax.ShapeDtypeStruct((heads, 5, rows, rows), jnp.float32),
        ),
        in_specs=[in_smem()] + in_vmem(9),
        out_specs=tuple(in_vmem(2)),
        scratch_shapes=[
            pltpu.VMEM((heads, 4, span, HEAD), jnp.bfloat16),
            pltpu.VMEM((heads, span, HEAD), jnp.bfloat16),
            pltpu.VMEM((heads, HEAD, rows), jnp.float32),
            pltpu.VMEM((heads, span, HEAD), jnp.float32),
            pltpu.VMEM((heads, span, HEAD), jnp.float32),
        ],
        compiler_params=pltpu.CompilerParams(vmem_limit_bytes=48 * 2**20),
        cost_estimate=pl.CostEstimate(
            flops=10 * heads * span * span * HEAD,
            bytes_accessed=20 * 2**20,
            transcendentals=heads * span * span,
        ),
        name="attention_backward",
    )(
        ranges,
        qkv_t,
        qkv,
        jnp.transpose(grad_output),
        grad_output,
        out_t,
        log_sums,
        sequence[:, None],
        sequence[None, :],
        tiles,
    )


def shards(
    x_in,
    grad_out,
    norm1_gain,
    qkv_weight,
    out_weight,
    bias_table,
    norm2_gain,
    router_weight,
    expert_in,
    expert_out,
    lengths,
    routes,
):
    tok_rows, model_width = x_in.shape
    heads_local = qkv_weight.shape[1] // (3 * HEAD)
    score_scale = HEAD ** (-0.5)
    tp_count = lax.axis_size("tp")
    dp_count = lax.axis_size("dp")
    normed_f, norm1_pull = jax.vjp(norm_apply, x_in, norm1_gain)
    normed_low = normed_f.astype(jnp.bfloat16)
    group_normed = gather_group(split_columns(normed_low))
    group_total = group_normed.shape[0]
    group_span = group_total // dp_count
    projected = sum_halves(row_product(group_normed, qkv_weight, False), group_span)
    kinds = jnp.arange(projected.shape[1], dtype=jnp.int32) // HEAD % 3
    qkv = (projected * jnp.where(kinds == 0, score_scale, 1.0)[None, :]).astype(jnp.bfloat16)
    qkv_t = jnp.transpose(qkv)
    sequence = segment_ids(lengths[0], group_span)
    head_start = lax.axis_index("tp") * heads_local
    table_heads = jnp.transpose(lax.dynamic_slice_in_dim(bias_table, head_start, heads_local, 1))
    block_rows = min(256, group_span)
    ranges = tile_ranges(lengths[0], sequence, block_rows)
    tiles = bias_tiles(table_heads, block_rows)
    attended, attended_t, log_sums = attention_forward(
        ranges, qkv_t, qkv, sequence, tiles, heads_local, block_rows
    )
    attended_group = gather_halves(attended)
    pair_rows = group_total // tp_count
    attn_cols = sum_blocks(row_product(attended_group, out_weight, False), pair_rows)
    hidden = x_in + join_rows(attn_cols)
    experts_count = lax.axis_size("ep")
    capacity = 2 * tok_rows // experts_count
    normed2_f, norm2_pull = jax.vjp(norm_apply, hidden, norm2_gain)
    normed2 = normed2_f.astype(jnp.bfloat16)
    logits = jnp.dot(normed2, router_weight, preferred_element_type=jnp.float32)
    shifted = jnp.exp(logits - jnp.max(logits, axis=1, keepdims=True))
    router = shifted / jnp.sum(shifted, axis=1, keepdims=True)
    route_int = (routes == jnp.arange(experts_count, dtype=jnp.int32)[None, :]).astype(jnp.int32)
    route_hot = route_int.astype(jnp.float32)
    gate = jnp.sum(router * route_hot, axis=1, keepdims=True)
    earlier = jnp.cumsum(route_int, axis=0) - route_int
    slot_index = jnp.sum(earlier * route_int, axis=1)
    position = routes[:, 0] * capacity + slot_index
    token_ids = jnp.arange(tok_rows, dtype=jnp.int32)
    slot_token = jnp.zeros((experts_count * capacity,), jnp.int32).at[position].set(token_ids)
    slot_live = jnp.zeros((experts_count * capacity, 1), jnp.bfloat16).at[position, 0].set(1.0)
    received = send_experts(jnp.take(normed2, slot_token, axis=0) * slot_live)
    full_in, full_out = (
        lax.all_gather(expert_in, ("tp", "dp"), axis=2, tiled=True),
        lax.all_gather(expert_out, ("tp", "dp"), axis=1, tiled=True),
    )
    pre_act = jnp.dot(received, full_in[0], preferred_element_type=jnp.float32)
    active_f, gelu_pull = jax.vjp(gelu_tanh, pre_act)
    active = active_f.astype(jnp.bfloat16)
    result_f = jnp.dot(active, full_out[0], preferred_element_type=jnp.float32)
    expert_tok = jnp.take(return_tokens(result_f.astype(jnp.bfloat16)), position, axis=0)
    out = hidden + gate * expert_tok.astype(jnp.float32)
    grad_result = (gate * grad_out).astype(jnp.bfloat16)
    grad_gate = jnp.sum(grad_out * expert_tok.astype(jnp.float32), axis=1, keepdims=True)
    grad_received = send_experts(jnp.take(grad_result, slot_token, axis=0) * slot_live)
    grad_active = contract_cols(grad_received, full_out[0])
    grad_pre = gelu_pull(grad_active)[0].astype(jnp.bfloat16)
    grad_first = contract_rows(active, grad_received)
    grad_second = contract_rows(grad_pre, received)
    stacked_in = jnp.concatenate([grad_first, grad_second], axis=1).astype(jnp.bfloat16)
    grad_sent = contract_cols(grad_pre, full_in[0])
    grad_expert_part = jnp.take(return_tokens(grad_sent.astype(jnp.bfloat16)), position, axis=0)
    grad_router_probs = grad_gate * route_hot
    grad_logits = (
        router * (grad_router_probs - jnp.sum(router * grad_router_probs, axis=1, keepdims=True))
    ).astype(jnp.bfloat16)
    grad_normed2 = grad_expert_part.astype(jnp.float32) + contract_cols(grad_logits, router_weight)
    grad_router = contract_rows(normed2, grad_logits)
    grad_hidden_norm, grad_gain_two = norm2_pull(grad_normed2)
    grad_hidden = grad_out + grad_hidden_norm
    grad_low = grad_hidden.astype(jnp.bfloat16)
    grad_attn_cols = gather_group(split_columns(grad_low))
    grad_attn_cols, stacked_in = lax.optimization_barrier((grad_attn_cols, stacked_in))
    grad_out_weight = contract_rows(attended_group, grad_attn_cols)
    grad_attended = sum_halves(row_product(grad_attn_cols, out_weight, True), group_span)
    grad_attended, stacked_in = lax.optimization_barrier(
        (grad_attended.astype(jnp.bfloat16), stacked_in)
    )
    stacked = lax.psum_scatter(stacked_in, ("tp", "dp"), scatter_dimension=0, tiled=True)
    grad_qkv, tile_sums = attention_backward(
        ranges,
        qkv_t,
        qkv,
        grad_attended,
        attended_t,
        log_sums,
        sequence,
        tiles,
        heads_local,
        block_rows,
    )
    grad_table_local = table_gradient(tile_sums, block_rows)
    grad_qkv, stacked = lax.optimization_barrier((grad_qkv, stacked))
    stacked = stacked.astype(jnp.float32)
    grad_weight_out = stacked[:, :model_width]
    grad_weight_in = jnp.transpose(stacked[:, model_width:])
    grad_qkv_group = gather_halves(grad_qkv)
    grad_qkv_weight = contract_rows(group_normed, grad_qkv_group)
    grad_normed = join_rows(sum_blocks(row_product(grad_qkv_group, qkv_weight, True), pair_rows))
    grad_x_norm, _ = norm1_pull(grad_normed)
    gain_part = jnp.sum(grad_qkv_weight * qkv_weight.astype(jnp.float32), axis=1)
    grad_gain_one = (
        lax.dynamic_update_slice(
            jnp.zeros((model_width,), jnp.float32),
            gain_part,
            (lax.axis_index("dp") * gain_part.shape[0],),
        )
        / norm1_gain
    )
    grad_in = grad_hidden + grad_x_norm
    table_full = lax.dynamic_update_slice(
        jnp.zeros(bias_table.shape, jnp.float32),
        jnp.transpose(grad_table_local),
        (jnp.int32(0), head_start),
    )
    grad_qkv_weight, grad_out_weight = (
        lax.psum(grad_qkv_weight.astype(jnp.bfloat16), "ep").astype(jnp.float32),
        lax.psum(grad_out_weight.astype(jnp.bfloat16), "ep").astype(jnp.float32),
    )
    grad_gain_one, grad_gain_two, grad_router, grad_table = lax.psum(
        (grad_gain_one, grad_gain_two, grad_router, table_full), ("ep", "tp", "dp")
    )
    return (
        out,
        grad_in,
        grad_gain_one,
        grad_qkv_weight,
        grad_out_weight,
        grad_table,
        grad_gain_two,
        grad_router,
        grad_weight_in[None],
        grad_weight_out[None],
    )


def solution(mesh):
    placed = (
        P(("ep", "tp", "dp"), None),
        P(("ep", "tp", "dp"), None),
        P(),
        P("dp", "tp"),
        P("tp", "dp"),
        P(),
        P(),
        P(),
        P("ep", None, ("tp", "dp")),
        P("ep", ("tp", "dp"), None),
        P(("ep", "dp"), None),
        P(("ep", "tp", "dp"), None),
    )
    return jax.shard_map(
        shards,
        mesh=mesh,
        in_specs=placed,
        out_specs=(
            P(("ep", "tp", "dp"), None),
            P(("ep", "tp", "dp"), None),
            P(),
            P("dp", "tp"),
            P("tp", "dp"),
            P(),
            P(),
            P(),
            P("ep", None, ("tp", "dp")),
            P("ep", ("tp", "dp"), None),
        ),
        check_vma=False,
    )
```
